128 devices in a mesh: seq: 64 (over y, z, x), head: 2 (over core).
Axes of the slice: x: 4, y: 4, z: 4, core: 2. Of those that a mesh axis runs over, the one named last changes fastest.
Arguments:
- query: bfloat16 [256, 4096], P('head'), may hold values from -16 to 16
- d_out: bfloat16 [256, 4096], P('head'), may hold values from -6144 to 6144
- out_fwd: bfloat16 [256, 4096], P('head'), may hold values from -6 to 6
- prompt_keys: bfloat16 [65536, 2048], P('seq', 'head'), may hold values from -16 to 16
- prompt_value_rows: bfloat16 [65536, 2048], P('seq', 'head'), may hold values from -6 to 6
- sibling_key_rows: bfloat16 [256, 2048], P('head'), may hold values from -5 to 5
- sibling_value_rows: bfloat16 [256, 2048], P('head'), may hold values from -6 to 6
- parents: int32 [8], replicated, may hold values from -1 to 6
Outputs:
- grad_query: bfloat16 [256, 4096], P('head')
- grad_prompt_keys: bfloat16 [65536, 2048], P('seq', 'head')
- grad_prompt_values: bfloat16 [65536, 2048], P('seq', 'head')
- grad_sib_keys: bfloat16 [256, 2048], P('head')
- grad_sib_values: bfloat16 [256, 2048], P('head')
The draws below stay inside these ranges and needn't reach their ends.
All inputs are finite; a program needn't handle non-finite values.
Results may differ from the reference program's by a relative error of at most 0.0054.
Values may be sent and summed in bfloat16 or wider, within the bound.
No kernel may reach another device: no remote copies, remote signals or barrier semaphores. Data moves between devices by JAX's collectives and lax.ppermute only.
A program may use at most 128 MiB of HBM per device.

```python
import jax
import jax.numpy as jnp
from jax import lax

STEPS = 8
STEP_LEN = 32
QUERY_HEADS = 32
KEY_VALUE_HEADS = 16
HEAD_DIMENSION = 128
SIBLING_TOKENS = 256
PROMPT_LENGTH = 65536


def draw_query(key, part):
    key = jax.random.fold_in(key, 5)
    sampled_values = jax.random.truncated_normal(key, -4.0, 4.0, (SIBLING_TOKENS, QUERY_HEADS * HEAD_DIMENSION), jnp.float32)
    return sampled_values.astype(jnp.bfloat16)


def draw_prompt_keys(key, part):
    key = jax.random.fold_in(key, 7)
    row_ramp = jnp.arange(PROMPT_LENGTH, dtype=jnp.float32) / (PROMPT_LENGTH - 1)
    sampled_values = jax.random.truncated_normal(key, -4.0, 4.0, (PROMPT_LENGTH, KEY_VALUE_HEADS * HEAD_DIMENSION), jnp.float32)
    sampled_values = sampled_values * (0.6 + 1.2 * row_ramp)[:, None]
    return sampled_values.astype(jnp.bfloat16)


def draw_parents(key, part):
    key = jax.random.fold_in(key, 9)
    step_ids = jnp.arange(STEPS, dtype=jnp.int32)
    drawn_ids = jax.random.randint(key, (STEPS,), 0, jnp.maximum(step_ids, 1))
    chosen = jnp.where(step_ids == 0, -1, drawn_ids).astype(jnp.int32)
    return chosen.at[STEPS - 1].set(STEPS - 2)


def block_scale(stream_key, dims, shards, low, top_value):
    loudness = 1.0
    for dim, shards_of in shards:
        heights = jax.random.uniform(jax.random.fold_in(jax.random.fold_in(stream_key, 6), dim), (shards_of,), jnp.float32, low / len(shards), top_value / len(shards))
        loudness = loudness * jnp.repeat(jnp.exp(heights), dims[dim] // shards_of).reshape((-1,) + (1,) * (len(dims) - 1 - dim))
    return loudness


def normal_values(rng, dims, scale, limit, split=(), kind=jnp.bfloat16):
    values = scale * jax.random.normal(rng, dims, jnp.float32)
    if split:
        values = values * block_scale(rng, dims, split, -0.22, 0.18)
    return jnp.clip(values, -limit, limit).astype(kind)


def setup_inputs(seed: int = 0) -> dict:
    arg_keys = jax.random.split(jax.random.key(seed), 9)
    query = draw_query(jax.random.fold_in(arg_keys[8], 71), 0)
    d_out = normal_values(arg_keys[1], (SIBLING_TOKENS, QUERY_HEADS * HEAD_DIMENSION), 1024.0, 6144.0, ((0, 2),))
    out_fwd = normal_values(arg_keys[2], (SIBLING_TOKENS, QUERY_HEADS * HEAD_DIMENSION), 1.0, 6.0, ((0, 2),))
    prompt_keys = draw_prompt_keys(jax.random.fold_in(arg_keys[8], 71), 0)
    prompt_value_rows = normal_values(arg_keys[4], (PROMPT_LENGTH, KEY_VALUE_HEADS * HEAD_DIMENSION), 1.0, 6.0, ((0, 64), (1, 2)))
    sibling_key_rows = normal_values(arg_keys[5], (SIBLING_TOKENS, KEY_VALUE_HEADS * HEAD_DIMENSION), 1.5, 5.0, ((0, 2),))
    sibling_value_rows = normal_values(arg_keys[6], (SIBLING_TOKENS, KEY_VALUE_HEADS * HEAD_DIMENSION), 1.0, 6.0, ((0, 2),))
    parents = draw_parents(jax.random.fold_in(arg_keys[8], 71), 0)
    return dict(query=query, d_out=d_out, out_fwd=out_fwd, prompt_keys=prompt_keys, prompt_value_rows=prompt_value_rows, sibling_key_rows=sibling_key_rows, sibling_value_rows=sibling_value_rows, parents=parents)


score_scale = 144.0 ** -0.5


def ancestry(parents):
    count = parents.shape[0]
    identity = jnp.eye(count, dtype=jnp.float32)
    link_mat = (parents[:, None] == jnp.arange(count, dtype=jnp.int32)[None, :]).astype(jnp.float32)
    reached = identity
    for turn_idx in range(count):
        reached = jnp.minimum(1.0, identity + jnp.dot(link_mat, reached, precision=lax.Precision.HIGHEST))
    return reached


def tree_mask(parents, step_len):
    reached = ancestry(parents) > 0.5
    total_tok = parents.shape[0] * step_len
    position = jnp.arange(total_tok, dtype=jnp.int32)
    step_of = position // step_len
    in_step = position % step_len
    same_step = step_of[:, None] == step_of[None, :]
    return reached[step_of[:, None], step_of[None, :]] & (jnp.logical_not(same_step) | (in_step[None, :] <= in_step[:, None]))


def reference(query, d_out, out_fwd, prompt_keys, prompt_value_rows, sibling_key_rows, sibling_value_rows, parents):
    heads_per_group = QUERY_HEADS // KEY_VALUE_HEADS
    allowed = tree_mask(parents, STEP_LEN)
    key_mask = allowed[:, None, :]

    def split_queries(input_array):
        return input_array.reshape(SIBLING_TOKENS, KEY_VALUE_HEADS, heads_per_group, HEAD_DIMENSION).transpose(1, 0, 2, 3)

    def split_keys(input_array):
        return input_array.reshape(input_array.shape[0], KEY_VALUE_HEADS, HEAD_DIMENSION).transpose(1, 0, 2)

    def one_group(inputs):
        q_head, do_head, o_head, kp_head, vp_head, ks_head, vs_head = [x.astype(jnp.float32) for x in inputs]
        prompt_scores = score_scale * jnp.einsum('tgd,rd->tgr', q_head, kp_head)
        sib_scores = score_scale * jnp.einsum('tgd,ud->tgu', q_head, ks_head)
        masked = jnp.where(key_mask, sib_scores, -jnp.inf)
        row_top = jnp.maximum(prompt_scores.max(-1), masked.max(-1))
        row_total = jnp.exp(prompt_scores - row_top[..., None]).sum(-1) + jnp.exp(masked - row_top[..., None]).sum(-1)
        log_total = row_top + jnp.log(row_total)
        out_dot = jnp.sum(do_head * o_head, axis=-1)
        prompt_probs = jnp.exp(prompt_scores - log_total[..., None])
        sib_probs = jnp.exp(masked - log_total[..., None])
        prompt_dp = jnp.einsum('tgd,rd->tgr', do_head, vp_head)
        sib_dp = jnp.einsum('tgd,ud->tgu', do_head, vs_head)
        prompt_ds = (prompt_probs * (prompt_dp - out_dot[..., None])).astype(jnp.bfloat16).astype(jnp.float32)
        sib_ds = (sib_probs * (sib_dp - out_dot[..., None])).astype(jnp.bfloat16).astype(jnp.float32)
        prompt_pb = prompt_probs.astype(jnp.bfloat16).astype(jnp.float32)
        sib_pb = sib_probs.astype(jnp.bfloat16).astype(jnp.float32)
        grad_q = jnp.einsum('tgr,rd->tgd', prompt_ds, kp_head) + jnp.einsum('tgu,ud->tgd', sib_ds, ks_head)
        grad_q = (score_scale * grad_q).astype(jnp.bfloat16)
        grad_kp = (score_scale * jnp.einsum('tgr,tgd->rd', prompt_ds, q_head)).astype(jnp.bfloat16)
        grad_vp = jnp.einsum('tgr,tgd->rd', prompt_pb, do_head).astype(jnp.bfloat16)
        grad_ks = (score_scale * jnp.einsum('tgu,tgd->ud', sib_ds, q_head)).astype(jnp.bfloat16)
        grad_vs = jnp.einsum('tgu,tgd->ud', sib_pb, do_head).astype(jnp.bfloat16)
        return grad_q, grad_kp, grad_vp, grad_ks, grad_vs

    grad_q, grad_kp, grad_vp, grad_ks, grad_vs = lax.map(one_group, (split_queries(query), split_queries(d_out), split_queries(out_fwd), split_keys(prompt_keys), split_keys(prompt_value_rows), split_keys(sibling_key_rows), split_keys(sibling_value_rows)))

    def join_keys(input_array):
        return input_array.transpose(1, 0, 2).reshape(input_array.shape[1], KEY_VALUE_HEADS * HEAD_DIMENSION)

    grad_query = grad_q.transpose(1, 0, 2, 3).reshape(SIBLING_TOKENS, QUERY_HEADS * HEAD_DIMENSION)
    return grad_query, join_keys(grad_kp), join_keys(grad_vp), join_keys(grad_ks), join_keys(grad_vs)
```

```python
import functools
import math

import jax
import jax.numpy as jnp
from jax import lax
from jax.experimental import pallas as pl
from jax.experimental.pallas import tpu as pltpu
from jax.sharding import PartitionSpec as P

f32 = jnp.float32
bf16 = jnp.bfloat16

D = 128
GROUP = 2
STEP_LEN = 32
SCALE = 144.0 ** (-0.5)
SCALE2 = SCALE * math.log2(math.e)
MASKED = -1e30
TOTAL_LOW, TOTAL_HIGH = 2.0**-60, 2.0**60
SWAP = [(0, 1), (1, 0)]
RADIX = 4
PAIR = 2
VMEM_LIMIT = 20 * 1024 * 1024

CHUNK = 2 * STEP_LEN
STAT_ROWS = 16


def dot_nt(a, b):
    return lax.dot_general(a, b, (((1,), (1,)), ((), ())), preferred_element_type=f32)


def dot_tn(a, b):
    return lax.dot_general(a, b, (((0,), (0,)), ((), ())), preferred_element_type=f32)


def dot_nn(a, b):
    return jnp.dot(a, b, preferred_element_type=f32)


def fold8(x, op):
    return op(x.reshape(x.shape[0] // 8, 8, x.shape[1]), axis=0)


def head_columns(head, width):
    return pl.ds(pl.multiple_of(head * width, width), width)


def head_rows(own, other, head):
    at = head_columns(head, GROUP * D)
    mine, theirs = own[:, at], other[:, at]
    return jnp.concatenate([x[:, g * D : (g + 1) * D] for g in range(GROUP) for x in (mine, theirs)], axis=0)


def out_dot_kernel(do, o, out):
    ones = jnp.ones((8, D), bf16)
    for head in range(out.shape[0]):
        at = slice(head * D, (head + 1) * D)
        product = do[:, at].astype(f32) * o[:, at].astype(f32)
        high = product.astype(bf16)
        low = (product - high.astype(f32)).astype(bf16)
        out[head : head + 1, :] = (dot_nt(ones, high) + dot_nt(ones, low))[0:1]


def finish_head(keys, probs, dprobs, out_dot, reference, probs_ref, ds_ref, pay_ref, stat_ref, head, k0):
    rows = probs.shape[1]
    probs_ref[head] = probs.astype(bf16)
    dscores = (probs * (dprobs - out_dot)).astype(bf16)
    ds_ref[head] = dscores
    total = jnp.sum(fold8(probs, jnp.sum), axis=0, keepdims=True)
    grad = dot_tn(keys, dscores).T.astype(bf16)
    stat_ref[0, pl.ds(head, 1), :] = reference
    stat_ref[1, pl.ds(head, 1), :] = total
    high = total.astype(bf16).astype(f32)
    stats = [reference, high, total - high]
    for g in range(GROUP):
        own, other = g * 2 * D, (g * 2 + 1) * D
        parts = [x[:, at : at + D] for at in (own, other) for x in stats]
        block = jnp.concatenate(parts + [jnp.zeros((STAT_ROWS - len(parts), D), f32)], axis=0).astype(bf16)
        for blk in range(D // STEP_LEN):
            k, at = k0 + g * (D // STEP_LEN) + blk, blk * STEP_LEN
            pay_ref[k, 0:STEP_LEN, :] = grad[own + at : own + at + STEP_LEN]
            pay_ref[k, STEP_LEN:CHUNK, :] = grad[other + at : other + at + STEP_LEN]
            pay_ref[k, CHUNK:, :] = block
    return total


def attend(keys, values, q_rows, do_rows, out_dot, mask, probs_ref, ds_ref, pay_ref, stat_ref, head, k0):
    rows = q_rows.shape[0]

    def masked(scores):
        return scores if mask is None else jnp.where(mask, scores, MASKED)

    def run(reference):
        scores = masked(dot_nt(keys, q_rows)) * SCALE2
        probs = jnp.exp2(scores if reference is None else scores - reference)
        held = jnp.zeros((1, rows), f32) if reference is None else reference
        return finish_head(
            keys, probs, dot_nt(values, do_rows), out_dot, held, probs_ref, ds_ref, pay_ref, stat_ref, head, k0
        )

    total = run(None)
    in_range = (jnp.min(total) > TOTAL_LOW) & (jnp.max(total) < TOTAL_HIGH)

    @pl.when(jnp.logical_not(in_range))
    def _():
        top = jnp.max(fold8(masked(dot_nt(keys, q_rows)), jnp.max), axis=0, keepdims=True)
        run((top * SCALE2).astype(bf16).astype(f32))


def row_dots(own, other, head):
    parts = [x[pl.ds(GROUP * head + g, 1), :] for g in range(GROUP) for x in (own, other)]
    return jnp.concatenate(parts, axis=1)


def prompt_kernel(place, q, qx, do, dox, dots, dotsx, kp, vp, probs, ds, pay, stat):
    kv = probs.shape[0]
    for i in range(PAIR):
        head = pl.program_id(0) * PAIR + i
        wide = place[1] * kv + head
        attend(
            kp[:, head_columns(head, D)],
            vp[:, head_columns(head, D)],
            head_rows(q, qx, wide),
            head_rows(do, dox, wide),
            row_dots(dots, dotsx, wide),
            None,
            probs,
            ds,
            pay,
            stat,
            head,
            i * (pay.shape[0] // PAIR),
        )


def sibling_mask(parents, core, half):
    steps = 2 * half // STEP_LEN
    reached = []
    for s in range(steps):
        bits = jnp.int32(1 << s)
        for t in range(s):
            bits = bits | jnp.where(parents[s] == t, reached[t], 0)
        reached.append(bits)

    def token(index):
        other_core = jnp.bitwise_xor((index // half) % 2, core)
        return other_core * (steps // 2) + (index % half) // STEP_LEN, index % STEP_LEN

    row_step, row_at = token(lax.broadcasted_iota(jnp.int32, (1, 2 * GROUP * half), 1))
    key_step, key_at = token(lax.broadcasted_iota(jnp.int32, (2 * half, 1), 0))
    row_bits = jnp.zeros(row_step.shape, jnp.int32)
    for s in range(steps):
        row_bits = jnp.where(row_step == s, reached[s], row_bits)
    seen = jnp.bitwise_and(jnp.right_shift(row_bits, key_step), 1) > 0
    return seen & ((key_step != row_step) | (key_at <= row_at))


def sibling_kernel(place, parents, q, qx, do, dox, dots, dotsx, ks, ksx, vs, vsx, probs, ds, pay, stat):
    kv = probs.shape[0]
    mask = sibling_mask(parents, place[1], ks.shape[0])
    for i in range(PAIR):
        head = pl.program_id(0) * PAIR + i
        wide = place[1] * kv + head
        at = head_columns(wide, D)
        attend(
            jnp.concatenate([ks[:, at], ksx[:, at]], axis=0),
            jnp.concatenate([vs[:, at], vsx[:, at]], axis=0),
            head_rows(q, qx, wide),
            head_rows(do, dox, wide),
            row_dots(dots, dotsx, wide),
            mask,
            probs,
            ds,
            pay,
            stat,
            head,
            i * (pay.shape[0] // PAIR),
        )


def merge_kernel(place, got, mine, out, weight):
    seq, core = place[0], place[1]
    sources = got.shape[0]
    at = pl.ds(pl.multiple_of((seq % (D // STEP_LEN)) * STEP_LEN, STEP_LEN), STEP_LEN)
    stats = got[:, CHUNK:, :].astype(f32)
    sib = mine[0, CHUNK:, :].astype(f32)
    sums = []
    for half in range(2):
        r = 3 * half
        reference, total = stats[:, r, :], stats[:, r + 1, :] + stats[:, r + 2, :]
        sib_reference, sib_total = sib[r : r + 1], sib[r + 1 : r + 2] + sib[r + 2 : r + 3]
        top = jnp.maximum(jnp.max(reference, axis=0, keepdims=True), sib_reference)
        row_total = jnp.sum(jnp.exp2(reference - top) * total, axis=0, keepdims=True) + jnp.exp2(sib_reference - top) * sib_total
        log_total = top + jnp.log2(row_total)
        weight[half] = jnp.concatenate(
            [
                SCALE * jnp.exp2(reference - log_total),
                SCALE * jnp.exp2(sib_reference - log_total),
                jnp.zeros((D - sources - 1, D), f32),
            ],
            axis=0,
        ).T
        weights = weight[half, at, :]
        rows = slice(half * STEP_LEN, (half + 1) * STEP_LEN)
        acc = weights[:, sources : sources + 1] * mine[0, rows, :].astype(f32)
        for i in range(sources):
            acc = acc + weights[:, i : i + 1] * got[i, rows, :].astype(f32)
        sums.append(acc)
    own, other = sums
    first = jnp.where(core == 0, own, other).astype(bf16)
    second = jnp.where(core == 0, other, own).astype(bf16)
    for i in range(sources):
        out[2 * i] = first
        out[2 * i + 1] = second


def key_grad_kernel(place, log_total, stat, probs, ds, q, qx, do, dox, grad_k, grad_v):
    kv = probs.shape[0]
    for i in range(PAIR):
        head = pl.program_id(0) * PAIR + i
        wide = place[1] * kv + head
        factor = jnp.exp2(stat[0, pl.ds(head, 1), :] - log_total[pl.ds(head, 1), :])
        factor = jnp.broadcast_to(factor, (D, factor.shape[1])).T
        q_rows = (head_rows(q, qx, wide).astype(f32) * (SCALE * factor)).astype(bf16)
        do_rows = (head_rows(do, dox, wide).astype(f32) * factor).astype(bf16)
        at = slice(i * D, (i + 1) * D)
        grad_k[:, at] = dot_nn(ds[head], q_rows).astype(bf16)
        grad_v[:, at] = dot_nn(probs[head], do_rows).astype(bf16)


def assemble_kernel(place, got, ks, ksx, vs, vsx, grad_q, grad_ks, grad_vs):
    kv, group, _, cores = got.shape[:4]
    for c in range(cores):
        for n in range(kv):
            for g in range(group):
                at = ((c * kv + n) * group + g) * D
                grad_q[:, at : at + D] = got[n, g, 0, c]
    width = ks.shape[1]

    @pl.when(place[1] == 0)
    def _():
        grad_ks[:, :width], grad_ks[:, width:] = ks[...], ksx[...]
        grad_vs[:, :width], grad_vs[:, width:] = vs[...], vsx[...]

    @pl.when(place[1] != 0)
    def _():
        grad_ks[:, :width], grad_ks[:, width:] = ksx[...], ks[...]
        grad_vs[:, :width], grad_vs[:, width:] = vsx[...], vs[...]


def combine(parts):
    top = functools.reduce(jnp.maximum, [x[0] for x in parts])
    return jnp.stack([top, sum(x[1] * jnp.exp2(x[0] - top) for x in parts)])


def total_over_seq(stat, size):
    stride = 1
    while stride < size:

        def moved(i, d):
            at = (i // stride) % RADIX
            return i + ((at + d) % RADIX - at) * stride

        others = [lax.ppermute(stat, "seq", [(i, moved(i, d)) for i in range(size)]) for d in range(1, RADIX)]
        stat = combine([stat] + others)
        stride *= RADIX
    return stat


def in_vmem(*arrays):
    return [pltpu.with_memory_space_constraint(x, pltpu.VMEM) for x in arrays]


def local(query, d_out, out_fwd, prompt_keys, prompt_value_rows, sibling_key_rows, sibling_value_rows, parents):
    seq, core = lax.axis_index("seq"), lax.axis_index("head")
    place = jnp.stack([seq, core]).astype(jnp.int32)
    devices = lax.axis_size("seq")
    kv = prompt_keys.shape[1] // D
    count = prompt_keys.shape[0]
    tokens = query.shape[0]
    rows = 2 * GROUP * tokens
    chunks = devices // kv
    blocks = tokens // STEP_LEN
    params = pltpu.CompilerParams(vmem_limit_bytes=VMEM_LIMIT, dimension_semantics=("arbitrary",))
    whole = pl.BlockSpec(memory_space=pltpu.VMEM)

    def swap(x):
        return lax.ppermute(x, "head", SWAP)

    qx, dox = swap(query), swap(d_out)
    dots = pl.pallas_call(
        out_dot_kernel,
        in_specs=[whole] * 2,
        out_specs=whole,
        out_shape=jax.ShapeDtypeStruct((query.shape[1] // D, tokens), f32),
        compiler_params=pltpu.CompilerParams(vmem_limit_bytes=VMEM_LIMIT),
        name="out_dot",
    )(d_out, out_fwd)
    dotsx = swap(dots)
    ksx, vsx = swap(sibling_key_rows), swap(sibling_value_rows)
    q_args = in_vmem(query, qx, d_out, dox)

    def attend_call(kernel, keys, prefetch, args, name):
        return pl.pallas_call(
            kernel,
            grid_spec=pltpu.PrefetchScalarGridSpec(
                num_scalar_prefetch=len(prefetch),
                grid=(kv // PAIR,),
                in_specs=[whole] * len(args),
                out_specs=[
                    whole,
                    whole,
                    pl.BlockSpec((chunks * PAIR, CHUNK + STAT_ROWS, D), lambda n, *_: (n, 0, 0)),
                    whole,
                ],
            ),
            out_shape=[
                pltpu.VMEM((kv, keys, rows), bf16),
                pltpu.VMEM((kv, keys, rows), bf16),
                jax.ShapeDtypeStruct((devices, CHUNK + STAT_ROWS, D), bf16),
                pltpu.VMEM((2, kv, rows), f32),
            ],
            compiler_params=params,
            cost_estimate=pl.CostEstimate(
                flops=6 * kv * keys * rows * D, bytes_accessed=4 * kv * keys * rows, transcendentals=kv * keys * rows
            ),
            name=name,
        )(*prefetch, *args)

    head_args = q_args + in_vmem(dots, dotsx)
    probs, ds, pay, stat = attend_call(
        prompt_kernel, count, (place,), head_args + in_vmem(prompt_keys, prompt_value_rows), "prompt"
    )
    got = lax.all_to_all(pay, "seq", split_axis=0, concat_axis=0, tiled=True)
    sib_probs, sib_ds, sib_pay, sib_stat = attend_call(
        sibling_kernel,
        2 * tokens,
        (place, parents),
        head_args + in_vmem(sibling_key_rows, ksx, sibling_value_rows, vsx),
        "sibling",
    )
    stats = combine([total_over_seq(stat, devices), sib_stat])
    log_total = stats[0] + jnp.log2(stats[1])

    merged = pl.pallas_call(
        merge_kernel,
        grid_spec=pltpu.PrefetchScalarGridSpec(
            num_scalar_prefetch=1,
            grid=(1,),
            in_specs=[
                pl.BlockSpec((devices, CHUNK + STAT_ROWS, D), lambda n, p: (0, 0, 0)),
                pl.BlockSpec((1, CHUNK + STAT_ROWS, D), lambda n, p: (p[0], 0, 0)),
            ],
            out_specs=pl.BlockSpec((2 * devices, STEP_LEN, D), lambda n, p: (0, 0, 0)),
            scratch_shapes=[pltpu.VMEM((2, D, D), f32)],
        ),
        out_shape=jax.ShapeDtypeStruct((2 * devices, STEP_LEN, D), bf16),
        compiler_params=params,
        name="merge",
    )(place, got, sib_pay)
    grad_q = lax.all_to_all(merged, ("seq", "head"), split_axis=0, concat_axis=0, tiled=True)

    def grad_call(keys, stat, probs, ds, name):
        return pl.pallas_call(
            key_grad_kernel,
            grid_spec=pltpu.PrefetchScalarGridSpec(
                num_scalar_prefetch=1,
                grid=(kv // PAIR,),
                in_specs=[whole] * 8,
                out_specs=[pl.BlockSpec((keys, PAIR * D), lambda n, *_: (0, n))] * 2,
            ),
            out_shape=[jax.ShapeDtypeStruct((keys, kv * D), bf16)] * 2,
            compiler_params=params,
            cost_estimate=pl.CostEstimate(
                flops=4 * kv * keys * rows * D, bytes_accessed=4 * kv * keys * rows, transcendentals=0
            ),
            name=name,
        )(place, *in_vmem(log_total, stat, probs, ds), *q_args)

    grad_ks, grad_vs = grad_call(2 * tokens, sib_stat, sib_probs, sib_ds, "sibling_grads")
    ks_other, vs_other = swap(grad_ks[tokens:]), swap(grad_vs[tokens:])
    grad_kp, grad_vp = grad_call(count, stat, probs, ds, "prompt_grads")

    half_spec = pl.BlockSpec((STEP_LEN, kv * D), lambda n, *_: (n, 0))
    grad_q, grad_ks, grad_vs = pl.pallas_call(
        assemble_kernel,
        grid_spec=pltpu.PrefetchScalarGridSpec(
            num_scalar_prefetch=1,
            grid=(blocks,),
            in_specs=[pl.BlockSpec((kv, GROUP, 1, 2, STEP_LEN, D), lambda n, *_: (0, 0, n, 0, 0, 0))] + [half_spec] * 4,
            out_specs=[
                pl.BlockSpec((STEP_LEN, query.shape[1]), lambda n, *_: (n, 0)),
                pl.BlockSpec((STEP_LEN, 2 * kv * D), lambda n, *_: (n, 0)),
                pl.BlockSpec((STEP_LEN, 2 * kv * D), lambda n, *_: (n, 0)),
            ],
        ),
        out_shape=[
            jax.ShapeDtypeStruct(query.shape, bf16),
            jax.ShapeDtypeStruct((tokens, 2 * kv * D), bf16),
            jax.ShapeDtypeStruct((tokens, 2 * kv * D), bf16),
        ],
        compiler_params=params,
        name="assemble",
    )(place, grad_q.reshape(kv, GROUP, blocks, 2, STEP_LEN, D), grad_ks, ks_other, grad_vs, vs_other)
    return grad_q, grad_kp, grad_vp, grad_ks, grad_vs


def solution(mesh):
    in_specs = (
        P("head", None),
        P("head", None),
        P("head", None),
        P("seq", "head"),
        P("seq", "head"),
        P("head", None),
        P("head", None),
        P(),
    )
    out_specs = (
        P("head", None),
        P("seq", "head"),
        P("seq", "head"),
        P("head", None),
        P("head", None),
    )
    return jax.shard_map(local, mesh=mesh, in_specs=in_specs, out_specs=out_specs, check_vma=False)
```

```python
import functools
import math

import jax
import jax.numpy as jnp
from jax import lax
from jax.experimental import pallas as pl
from jax.experimental.pallas import tpu as pltpu
from jax.sharding import PartitionSpec as P

f32 = jnp.float32
bf16 = jnp.bfloat16

D = 128
GROUP = 2
STEP_LEN = 32
SCALE = 144.0 ** (-0.5)
SCALE2 = SCALE * math.log2(math.e)
MASKED = -1e30
TOTAL_LOW, TOTAL_HIGH = 2.0**-60, 2.0**60
SWAP = [(0, 1), (1, 0)]
RADIX = 4
PAIR = 2
VMEM_LIMIT = 20 * 1024 * 1024

CHUNK = 2 * STEP_LEN
STAT_ROWS = 16


def dot_nt(a, b):
    return lax.dot_general(a, b, (((1,), (1,)), ((), ())), preferred_element_type=f32)


def dot_tn(a, b):
    return lax.dot_general(a, b, (((0,), (0,)), ((), ())), preferred_element_type=f32)


def dot_nn(a, b):
    return jnp.dot(a, b, preferred_element_type=f32)


def fold8(x, op):
    return op(x.reshape(x.shape[0] // 8, 8, x.shape[1]), axis=0)


def head_rows(own, other, i):
    cols = [slice((GROUP * i + g) * D, (GROUP * i + g + 1) * D) for g in range(GROUP)]
    return jnp.concatenate([x[:, at] for at in cols for x in (own, other)], axis=0)


def out_dot_kernel(do, o, out):
    ones = jnp.ones((8, D), bf16)
    for head in range(out.shape[0]):
        at = slice(head * D, (head + 1) * D)
        product = do[:, at].astype(f32) * o[:, at].astype(f32)
        high = product.astype(bf16)
        low = (product - high.astype(f32)).astype(bf16)
        out[head : head + 1, :] = (dot_nt(ones, high) + dot_nt(ones, low))[0:1]


def attend(keys, values, q_rows, do_rows, out_dot, mask, pay_ref, stat_ref, head, k0):
    rows = q_rows.shape[0]

    def masked(scores):
        return scores if mask is None else jnp.where(mask, scores, MASKED)

    def run(reference):
        scores = masked(dot_nt(keys, q_rows)) * SCALE2
        probs = jnp.exp2(scores if reference is None else scores - reference)
        dscores = (probs * (dot_nt(values, do_rows) - out_dot)).astype(bf16)
        total = jnp.sum(fold8(probs, jnp.sum), axis=0, keepdims=True)
        grad = dot_tn(keys, dscores).T.astype(bf16)
        held = jnp.zeros((1, rows), f32) if reference is None else reference
        stat_ref[0, pl.ds(head, 1), :] = held
        stat_ref[1, pl.ds(head, 1), :] = total
        high = total.astype(bf16).astype(f32)
        stats = [held, high, total - high]
        for g in range(GROUP):
            own, other = g * 2 * D, (g * 2 + 1) * D
            parts = [x[:, at : at + D] for at in (own, other) for x in stats]
            block = jnp.concatenate(parts + [jnp.zeros((STAT_ROWS - len(parts), D), f32)], axis=0).astype(bf16)
            for blk in range(D // STEP_LEN):
                k, at = k0 + g * (D // STEP_LEN) + blk, blk * STEP_LEN
                pay_ref[k, 0:STEP_LEN, :] = grad[own + at : own + at + STEP_LEN]
                pay_ref[k, STEP_LEN:CHUNK, :] = grad[other + at : other + at + STEP_LEN]
                pay_ref[k, CHUNK:, :] = block
        return total

    total = run(None)
    in_range = (jnp.min(total) > TOTAL_LOW) & (jnp.max(total) < TOTAL_HIGH)

    @pl.when(jnp.logical_not(in_range))
    def _():
        top = jnp.max(fold8(masked(dot_nt(keys, q_rows)), jnp.max), axis=0, keepdims=True)
        run((top * SCALE2).astype(bf16).astype(f32))


def key_grads(keys, values, q_rows, do_rows, out_dot, mask, log_total):
    scores = dot_nt(keys, q_rows)
    if mask is not None:
        scores = jnp.where(mask, scores, MASKED)
    probs = jnp.exp2(scores * SCALE2 - log_total)
    dscores = (probs * (dot_nt(values, do_rows) - out_dot)).astype(bf16)
    grad_k = (SCALE * dot_nn(dscores, q_rows)).astype(bf16)
    return grad_k, dot_nn(probs.astype(bf16), do_rows).astype(bf16)


def row_dots(own, other, head):
    parts = [x[pl.ds(GROUP * head + g, 1), :] for g in range(GROUP) for x in (own, other)]
    return jnp.concatenate(parts, axis=1)


def heads_of_step(kv, core, q, qx, do, dox, dots, dotsx):
    for i in range(PAIR):
        head = pl.program_id(0) * PAIR + i
        yield i, head, head_rows(q, qx, i), head_rows(do, dox, i), row_dots(dots, dotsx, core * kv + head)


def prompt_kernel(place, q, qx, do, dox, dots, dotsx, kp, vp, pay, stat):
    kv = stat.shape[1]
    for i, head, q_rows, do_rows, out_dot in heads_of_step(kv, place[1], q, qx, do, dox, dots, dotsx):
        at = slice(i * D, (i + 1) * D)
        attend(kp[:, at], vp[:, at], q_rows, do_rows, out_dot, None, pay, stat, head, i * (pay.shape[0] // PAIR))


def prompt_grads_kernel(place, log_total, q, qx, do, dox, dots, dotsx, kp, vp, grad_k, grad_v):
    kv = log_total.shape[0]
    for i, head, q_rows, do_rows, out_dot in heads_of_step(kv, place[1], q, qx, do, dox, dots, dotsx):
        at = slice(i * D, (i + 1) * D)
        grad_k[:, at], grad_v[:, at] = key_grads(
            kp[:, at], vp[:, at], q_rows, do_rows, out_dot, None, log_total[pl.ds(head, 1), :]
        )


def sibling_mask(parents, core, half):
    steps = 2 * half // STEP_LEN
    reached = []
    for s in range(steps):
        bits = jnp.int32(1 << s)
        for t in range(s):
            bits = bits | jnp.where(parents[s] == t, reached[t], 0)
        reached.append(bits)

    def token(index):
        other_core = jnp.bitwise_xor((index // half) % 2, core)
        return other_core * (steps // 2) + (index % half) // STEP_LEN, index % STEP_LEN

    row_step, row_at = token(lax.broadcasted_iota(jnp.int32, (1, 2 * GROUP * half), 1))
    key_step, key_at = token(lax.broadcasted_iota(jnp.int32, (2 * half, 1), 0))
    row_bits = jnp.zeros(row_step.shape, jnp.int32)
    for s in range(steps):
        row_bits = jnp.where(row_step == s, reached[s], row_bits)
    seen = jnp.bitwise_and(jnp.right_shift(row_bits, key_step), 1) > 0
    return seen & ((key_step != row_step) | (key_at <= row_at))


def sibling_kernel(place, parents, q, qx, do, dox, dots, dotsx, ks, ksx, vs, vsx, pay, stat):
    kv = stat.shape[1]
    mask = sibling_mask(parents, place[1], ks.shape[0])
    for i, head, q_rows, do_rows, out_dot in heads_of_step(kv, place[1], q, qx, do, dox, dots, dotsx):
        at = slice(i * D, (i + 1) * D)
        keys = jnp.concatenate([ks[:, at], ksx[:, at]], axis=0)
        values = jnp.concatenate([vs[:, at], vsx[:, at]], axis=0)
        attend(keys, values, q_rows, do_rows, out_dot, mask, pay, stat, head, i * (pay.shape[0] // PAIR))


def sibling_grads_kernel(place, parents, log_total, q, qx, do, dox, dots, dotsx, ks, ksx, vs, vsx, gk, gkx, gv, gvx):
    kv = log_total.shape[0]
    half = ks.shape[0]
    mask = sibling_mask(parents, place[1], half)
    for i, head, q_rows, do_rows, out_dot in heads_of_step(kv, place[1], q, qx, do, dox, dots, dotsx):
        at = slice(i * D, (i + 1) * D)
        keys = jnp.concatenate([ks[:, at], ksx[:, at]], axis=0)
        values = jnp.concatenate([vs[:, at], vsx[:, at]], axis=0)
        grad_k, grad_v = key_grads(keys, values, q_rows, do_rows, out_dot, mask, log_total[pl.ds(head, 1), :])
        gk[:, at], gkx[:, at] = grad_k[:half], grad_k[half:]
        gv[:, at], gvx[:, at] = grad_v[:half], grad_v[half:]


def merge_kernel(place, got, mine, out, weight, total_ref):
    seq, core = place[0], place[1]
    sources = got.shape[0]
    at = pl.ds(pl.multiple_of((seq % (D // STEP_LEN)) * STEP_LEN, STEP_LEN), STEP_LEN)
    stats = got[:, CHUNK:, :].astype(f32)
    sib = mine[0, CHUNK:, :].astype(f32)
    plain = jnp.max(jnp.abs(jnp.concatenate([stats[:, 0], stats[:, 3], sib[0:1], sib[3:4]], axis=0))) == 0.0
    for half in range(2):
        r = 3 * half
        reference, total = stats[:, r, :], stats[:, r + 1, :] + stats[:, r + 2, :]
        sib_reference, sib_total = sib[r : r + 1], sib[r + 1 : r + 2] + sib[r + 2 : r + 3]
        top = jnp.maximum(jnp.max(reference, axis=0, keepdims=True), sib_reference)
        row_total = jnp.sum(jnp.exp2(reference - top) * total, axis=0, keepdims=True) + jnp.exp2(sib_reference - top) * sib_total
        log_total = top + jnp.log2(row_total)
        weight[half] = jnp.concatenate(
            [
                SCALE * jnp.exp2(reference - log_total),
                SCALE * jnp.exp2(sib_reference - log_total),
                jnp.zeros((D - sources - 1, D), f32),
            ],
            axis=0,
        ).T

    @pl.when(plain)
    def _():
        acc = mine[0, 0:CHUNK, :].astype(f32)
        for i in range(sources):
            acc = acc + got[i, 0:CHUNK, :].astype(f32)
        total_ref[0] = acc[:STEP_LEN] * weight[0, at, :][:, 0:1]
        total_ref[1] = acc[STEP_LEN:] * weight[1, at, :][:, 0:1]

    @pl.when(jnp.logical_not(plain))
    def _():
        for half in range(2):
            weights = weight[half, at, :]
            rows = slice(half * STEP_LEN, (half + 1) * STEP_LEN)
            acc = weights[:, sources : sources + 1] * mine[0, rows, :].astype(f32)
            for i in range(sources):
                acc = acc + weights[:, i : i + 1] * got[i, rows, :].astype(f32)
            total_ref[half] = acc

    own, other = total_ref[0], total_ref[1]
    first = jnp.where(core == 0, own, other).astype(bf16)
    second = jnp.where(core == 0, other, own).astype(bf16)
    for i in range(sources):
        out[2 * i] = first
        out[2 * i + 1] = second


def assemble_kernel(got, grad_q):
    kv, group, blocks, cores = got.shape[:4]
    blk = pl.program_id(0)
    for c in range(cores):
        for n in range(kv):
            for g in range(group):
                at = ((c * kv + n) * group + g) * D
                grad_q[:, at : at + D] = got[n, g, blk, c]


def join_kernel(place, ks, ksx, vs, vsx, grad_ks, grad_vs):
    width = ks.shape[1]

    @pl.when(place[1] == 0)
    def _():
        grad_ks[:, :width], grad_ks[:, width:] = ks[...], ksx[...]
        grad_vs[:, :width], grad_vs[:, width:] = vs[...], vsx[...]

    @pl.when(place[1] != 0)
    def _():
        grad_ks[:, :width], grad_ks[:, width:] = ksx[...], ks[...]
        grad_vs[:, :width], grad_vs[:, width:] = vsx[...], vs[...]


def combine(parts):
    top = functools.reduce(jnp.maximum, [x[0] for x in parts])
    return jnp.stack([top, sum(x[1] * jnp.exp2(x[0] - top) for x in parts)])


def total_over_seq(stat, size):
    stride = 1
    while stride < size:

        def moved(i, d):
            at = (i // stride) % RADIX
            return i + ((at + d) % RADIX - at) * stride

        others = [lax.ppermute(stat, "seq", [(i, moved(i, d)) for i in range(size)]) for d in range(1, RADIX)]
        stat = combine([stat] + others)
        stride *= RADIX
    return stat


def in_hbm(*arrays):
    return [pltpu.with_memory_space_constraint(x, pltpu.HBM) for x in arrays]


def local(query, d_out, out_fwd, prompt_keys, prompt_value_rows, sibling_key_rows, sibling_value_rows, parents):
    seq, core = lax.axis_index("seq"), lax.axis_index("head")
    place = jnp.stack([seq, core]).astype(jnp.int32)
    devices = lax.axis_size("seq")
    kv = prompt_keys.shape[1] // D
    count = prompt_keys.shape[0]
    tokens = query.shape[0]
    rows = 2 * GROUP * tokens
    chunks = devices // kv
    blocks = tokens // STEP_LEN
    steps = kv // PAIR
    params = pltpu.CompilerParams(vmem_limit_bytes=VMEM_LIMIT, dimension_semantics=("arbitrary",))
    whole = pl.BlockSpec(memory_space=pltpu.VMEM)
    bf = lambda *shape: jax.ShapeDtypeStruct(shape, bf16)

    def swap(x):
        return lax.ppermute(x, "head", SWAP)

    def call(kernel, name, prefetch, grid, in_specs, out_specs, out_shape, args, flops=0, exps=0, scratch=()):
        return pl.pallas_call(
            kernel,
            grid_spec=pltpu.PrefetchScalarGridSpec(
                num_scalar_prefetch=len(prefetch),
                grid=(grid,),
                in_specs=in_specs,
                out_specs=out_specs,
                scratch_shapes=scratch,
            ),
            out_shape=out_shape,
            compiler_params=params,
            cost_estimate=pl.CostEstimate(flops=flops, bytes_accessed=1 << 22, transcendentals=exps),
            name=name,
        )(*prefetch, *args)

    step_q = pl.BlockSpec((tokens, PAIR * GROUP * D), lambda n, p, *_: (0, p[1] * steps + n))
    step_k = pl.BlockSpec((tokens, PAIR * D), lambda n, p, *_: (0, p[1] * steps + n))
    step_cols = lambda size: pl.BlockSpec((size, PAIR * D), lambda n, *_: (0, n))

    qx, dox = swap(query), swap(d_out)
    dot_spec = pl.BlockSpec((tokens, 8 * D), lambda n: (0, n))
    dots = call(
        out_dot_kernel,
        "out_dot",
        (),
        query.shape[1] // (8 * D),
        [dot_spec] * 2,
        pl.BlockSpec((8, tokens), lambda n: (n, 0)),
        jax.ShapeDtypeStruct((query.shape[1] // D, tokens), f32),
        in_hbm(d_out, out_fwd),
    )
    dotsx = swap(dots)
    ksx, vsx = swap(sibling_key_rows), swap(sibling_value_rows)

    row_args = in_hbm(query, qx, d_out, dox) + [dots, dotsx]
    row_specs = [step_q] * 4 + [whole] * 2
    prompt_args = row_args + in_hbm(prompt_keys, prompt_value_rows)
    prompt_specs = row_specs + [step_cols(count)] * 2
    sib_args = row_args + in_hbm(sibling_key_rows, ksx, sibling_value_rows, vsx)
    sib_specs = row_specs + [step_k] * 4
    attend_specs = [
        pl.BlockSpec((chunks * PAIR, CHUNK + STAT_ROWS, D), lambda n, *_: (n, 0, 0)),
        whole,
    ]
    attend_shape = [bf(devices, CHUNK + STAT_ROWS, D), jax.ShapeDtypeStruct((2, kv, rows), f32)]
    work = kv * rows * D

    pay, stat = call(
        prompt_kernel,
        "prompt",
        (place,),
        steps,
        prompt_specs,
        attend_specs,
        attend_shape,
        prompt_args,
        6 * count * work,
        count * kv * rows,
    )
    got = lax.all_to_all(pay, "seq", split_axis=0, concat_axis=0, tiled=True)
    sib_pay, sib_stat = call(
        sibling_kernel,
        "sibling",
        (place, parents),
        steps,
        sib_specs,
        attend_specs,
        attend_shape,
        sib_args,
        12 * tokens * work,
        2 * tokens * kv * rows,
    )
    stats = combine([total_over_seq(stat, devices), sib_stat])
    log_total = stats[0] + jnp.log2(stats[1])
    got, log_total = lax.optimization_barrier((got, log_total))

    merged = call(
        merge_kernel,
        "merge",
        (place,),
        1,
        [
            pl.BlockSpec((devices, CHUNK + STAT_ROWS, D), lambda n, p: (0, 0, 0)),
            pl.BlockSpec((1, CHUNK + STAT_ROWS, D), lambda n, p: (p[0], 0, 0)),
        ],
        pl.BlockSpec((2 * devices, STEP_LEN, D), lambda n, p: (0, 0, 0)),
        bf(2 * devices, STEP_LEN, D),
        in_hbm(got, sib_pay),
        scratch=[pltpu.VMEM((2, D, D), f32), pltpu.VMEM((2, STEP_LEN, D), f32)],
    )
    grad_q = lax.all_to_all(merged, ("seq", "head"), split_axis=0, concat_axis=0, tiled=True)

    gks, gks_other, gvs, gvs_other = call(
        sibling_grads_kernel,
        "sibling_grads",
        (place, parents),
        steps,
        [whole] + sib_specs,
        [step_cols(tokens)] * 4,
        [bf(tokens, kv * D)] * 4,
        [log_total] + sib_args,
        16 * tokens * work,
        2 * tokens * kv * rows,
    )
    gks_other, gvs_other = swap(gks_other), swap(gvs_other)
    grad_kp, grad_vp = call(
        prompt_grads_kernel,
        "prompt_grads",
        (place,),
        steps,
        [whole] + prompt_specs,
        [step_cols(count)] * 2,
        [bf(count, kv * D)] * 2,
        [log_total] + prompt_args,
        8 * count * work,
        count * kv * rows,
    )
    grad_ks, grad_vs = call(
        join_kernel,
        "join",
        (place,),
        1,
        [pl.BlockSpec((tokens, kv * D), lambda n, *_: (0, 0))] * 4,
        [pl.BlockSpec((tokens, 2 * kv * D), lambda n, *_: (0, 0))] * 2,
        [bf(tokens, 2 * kv * D)] * 2,
        [gks, gks_other, gvs, gvs_other],
    )
    grad_q = call(
        assemble_kernel,
        "assemble",
        (),
        blocks,
        [pl.BlockSpec((kv, GROUP, blocks, 2, STEP_LEN, D), lambda n: (0, 0, 0, 0, 0, 0))],
        pl.BlockSpec((STEP_LEN, query.shape[1]), lambda n: (n, 0)),
        bf(*query.shape),
        in_hbm(grad_q.reshape(kv, GROUP, blocks, 2, STEP_LEN, D)),
    )
    return grad_q, grad_kp, grad_vp, grad_ks, grad_vs


def solution(mesh):
    in_specs = (
        P("head", None),
        P("head", None),
        P("head", None),
        P("seq", "head"),
        P("seq", "head"),
        P("head", None),
        P("head", None),
        P(),
    )
    out_specs = (
        P("head", None),
        P("seq", "head"),
        P("seq", "head"),
        P("head", None),
        P("head", None),
    )
    return jax.shard_map(local, mesh=mesh, in_specs=in_specs, out_specs=out_specs, check_vma=False)
```
